32 devices in a mesh: dom: 2 (over y), orb: 16 (over z, x, core).
Axes of the slice: x: 2, y: 2, z: 4, core: 2. Of those that a mesh axis runs over, the one named last changes fastest.
Arguments:
- orbitals: float32 [2, 16, 64, 64, 128], P('dom', 'orb'), may hold values from -6 to 6
- occupations: float32 [2, 16], P('dom', 'orb'), may hold values from 0.01 to 0.2
- core_density: float32 [2, 64, 4096], P('dom'), may hold values from 0.1 to 2
- ion_potential: float32 [2, 64, 4096], P('dom'), may hold values from -3 to 3
- neighbors: int32 [2, 2], replicated, may hold values from 0 to 1, as said below
- margin_widths: int32 [2, 2], replicated, may hold values from 1 to 8, as said below
Outputs:
- orbitals_out: float32 [2, 16, 64, 64, 128], P('dom', 'orb')
- potential: float32 [2, 64, 4096], P('dom', None, 'orb')
The draws below stay inside these ranges and needn't reach their ends.
Inputs may be any that keep to these rules, and one draw needn't show every extreme that they name: `neighbors`: each domain's left and right neighbours may be any domains, itself included, and two domains may share a neighbour. `margin_widths`: every draw has some entry equal to 8.
All inputs are finite; a program needn't handle non-finite values.
Results may differ from the reference program's by a relative error of at most 0.0001.
Values sent between devices are 32-bit elements; how exact they have to be, the bound alone decides.
A program may use at most 128 MiB of HBM per device.

```python
import math
import jax
import jax.numpy as jnp
from jax import lax

GRID = 64
BUFFER = 8
STEPS = 2
SPLITS = 1
ORBITALS = 16
DOMAINS = 2


def draw_neighbors(key, part):
    key_a = jax.random.fold_in(key, 11)
    key_b = jax.random.fold_in(key, 12)
    key_c = jax.random.fold_in(key, 13)
    entries = jax.random.randint(key_a, (DOMAINS * 2,), 0, DOMAINS)
    top_slot = jax.random.randint(key_b, (), 0, DOMAINS * 2)
    step_on = jax.random.randint(key_c, (), 1, DOMAINS * 2)
    low_slot = (top_slot + step_on) % (DOMAINS * 2)
    entries = entries.at[top_slot].set(DOMAINS - 1).at[low_slot].set(0)
    return entries.reshape(DOMAINS, 2).astype(jnp.int32)


def draw_margin_widths(key, part):
    key_a = jax.random.fold_in(key, 1)
    key_b = jax.random.fold_in(key, 2)
    entries = jax.random.randint(key_a, (DOMAINS * 2,), 1, BUFFER + 1)
    chosen = jax.random.randint(key_b, (), 0, DOMAINS * 2)
    entries = entries.at[chosen].set(BUFFER).at[(chosen + 1) % (DOMAINS * 2)].set(1)
    return entries.reshape(DOMAINS, 2).astype(jnp.int32)


def block_scale(rng, extent, pieces, smallest, high):
    level = 1.0
    for dim, blocks in pieces:
        steps = jax.random.uniform(jax.random.fold_in(jax.random.fold_in(rng, 6), dim), (blocks,), jnp.float32, smallest / len(pieces), high / len(pieces))
        level = level * jnp.repeat(jnp.exp(steps), extent[dim] // blocks).reshape((-1,) + (1,) * (len(extent) - 1 - dim))
    return level


def gaussian(own_key, extent, spread, limit, pieces=(), held_as=jnp.bfloat16):
    gain = block_scale(own_key, extent, pieces, -0.22, 0.18) if pieces else 1.0
    values = jax.random.normal(own_key, extent, jnp.float32) * spread * gain
    return jnp.minimum(jnp.maximum(values, -limit), limit).astype(held_as)


def setup_inputs(seed: int = 0) -> dict:
    key_of = jax.random.split(jax.random.key(seed), 7)
    orbitals = gaussian(key_of[0], (DOMAINS, ORBITALS, GRID, GRID, 2 * GRID), 1.0, 6.0, ((0, 2), (1, 16)), jnp.float32)
    occupations = jnp.clip(jnp.exp(math.log(0.2) - 2.9957323 * jax.random.uniform(key_of[1], (DOMAINS, ORBITALS), jnp.float32) ** block_scale(key_of[1], (DOMAINS, ORBITALS), ((0, 2), (1, 16)), -0.2, 0.2)), 0.01, 0.2)
    core_density = jnp.clip(jnp.exp(math.log(2.0) - 2.9957323 * jax.random.uniform(key_of[2], (DOMAINS, GRID, GRID * GRID), jnp.float32) ** block_scale(key_of[2], (DOMAINS, GRID, GRID * GRID), ((0, 2),), -0.2, 0.2)), 0.1, 2.0)
    ion_potential = gaussian(key_of[3], (DOMAINS, GRID, GRID * GRID), 0.5, 3.0, ((0, 2),), jnp.float32)
    neighbors = draw_neighbors(jax.random.fold_in(key_of[6], 71), 0)
    margin_widths = draw_margin_widths(jax.random.fold_in(key_of[6], 71), 0)
    return {"orbitals": orbitals, "occupations": occupations, "core_density": core_density, "ion_potential": ion_potential, "neighbors": neighbors, "margin_widths": margin_widths}


EXCHANGE_COEF = (3.0 / math.pi) ** (1.0 / 3.0)
TIME_STEP = 0.5


def laplace(states):
    lead = [(0, 0)] * (states.ndim - 4)
    padded = jnp.pad(states, lead + [(1, 1), (1, 1), (0, 0), (1, 1)])
    summed = padded[..., 2:, 1:-1, :, 1:-1] + padded[..., :-2, 1:-1, :, 1:-1]
    summed = summed + padded[..., 1:-1, 2:, :, 1:-1] + padded[..., 1:-1, :-2, :, 1:-1]
    summed = summed + padded[..., 1:-1, 1:-1, :, 2:] + padded[..., 1:-1, 1:-1, :, :-2]
    return summed - 6.0 * states


def kinetic(states, half_step):
    result = states
    current = states
    for degree in range(1, 5):
        applied = -0.5 * laplace(current)
        factor = half_step / degree
        current = jnp.stack([factor * applied[..., 1, :], -factor * applied[..., 0, :]], axis=-2)
        result = result + current
    return result


def rotate_phase(states, potential_cube):
    rotation = TIME_STEP * potential_cube
    cosine = jnp.cos(rotation)
    sine_val = jnp.sin(rotation)
    real_part = states[..., 0, :]
    imag_part = states[..., 1, :]
    return jnp.stack([cosine * real_part + sine_val * imag_part, cosine * imag_part - sine_val * real_part], axis=-2)


def propagate(states, potential_cube):
    for repeat in range(SPLITS):
        states = kinetic(states, 0.5 * TIME_STEP)
        states = rotate_phase(states, potential_cube)
        states = kinetic(states, 0.5 * TIME_STEP)
    return states


def density_terms(states, weights):
    squares = jnp.sum(states * states, axis=3)
    summed = jnp.sum(weights[:, None, None, None] * squares, axis=0)
    return summed.reshape(GRID, GRID * GRID)


def blend_rows(density_now, neighbors, margin_widths):
    from_left = density_now[neighbors[:, 0], GRID - BUFFER:]
    from_right = density_now[neighbors[:, 1], :BUFFER]
    plane_pos = jnp.arange(BUFFER).astype(jnp.float32)
    width_left = margin_widths[:, 0:1].astype(jnp.float32)
    width_right = margin_widths[:, 1:2].astype(jnp.float32)
    ramp_left = (jnp.maximum(width_left - plane_pos, 0.0) / (width_left + 1.0))[:, :, None]
    ramp_right = (jnp.maximum(plane_pos - (BUFFER - width_right) + 1.0, 0.0) / (width_right + 1.0))[:, :, None]
    lower_rows = (1.0 - ramp_left) * density_now[:, :BUFFER] + ramp_left * from_left
    upper_rows = (1.0 - ramp_right) * density_now[:, GRID - BUFFER:] + ramp_right * from_right
    return jnp.concatenate([lower_rows, density_now[:, BUFFER:GRID - BUFFER], upper_rows], axis=1)


def reference(orbitals, occupations, core_density, ion_potential, neighbors, margin_widths):
    states = orbitals.reshape(DOMAINS, ORBITALS, GRID, GRID, 2, GRID)
    potential = ion_potential
    for repeat in range(STEPS):
        density_now = lax.map(lambda packed: density_terms(packed[0], packed[1]), (states, occupations)) + core_density
        blended = blend_rows(density_now, neighbors, margin_widths)
        potential = ion_potential - EXCHANGE_COEF * jnp.cbrt(blended)
        states = lax.map(lambda packed: propagate(packed[0], packed[1].reshape(GRID, GRID, GRID)), (states, potential))
    return states.reshape(orbitals.shape), potential
```

```python
import functools
import math

import jax
import jax.numpy as jnp
from jax import lax
from jax.experimental import pallas as pl
from jax.experimental.pallas import tpu as pltpu
from jax.sharding import PartitionSpec as P

BUFFER = 8
STEPS = 2
CHUNKS = 4
GRID = 64
LANES = 128
EXCHANGE_COEF = (3.0 / math.pi) ** (1.0 / 3.0)
H = 0.125
MESH = pl.DeviceIdType.MESH


def kernel(
    n, doms,
    orb_ref, occ_ref, nbr_ref, wid_ref, core_hbm, ion_hbm,
    out_ref, pot_ref,
    psi, u1, u2, u3, core_v, ion_v,
    dens, vbuf, recv_a, recv_b, recv_c, edges_0, edges_1,
    load_sem,
    a_send, a_recv, b_send, b_recv, c_send, c_recv,
    d_send, d_recv, z_send, z_recv, x_send, x_recv, k_send, k_recv,
):
    half = n // 2
    far = n // 4
    r = GRID * GRID // (LANES * n)
    planes = GRID // CHUNKS
    rows = planes * r
    dom = lax.axis_index("dom")
    p = lax.axis_index("orb")
    c = lax.rem(p, 2)
    b = lax.rem(p // 2, 2)
    a = p // 4
    m = p // 2
    core_peer = p + 1 - 2 * c
    x_peer = p + 2 - 4 * b

    def z_peer(i):
        other = lax.rem(a + i, far)
        return other, other * 4 + b * 2 + c

    def d_peer(i):
        return lax.rem(dom + i, doms)

    barrier = pltpu.get_barrier_semaphore()
    peers = [(dom, core_peer), (dom, x_peer)]
    peers += [(dom, z_peer(i)[1]) for i in range(1, far)]
    peers += [(d_peer(i), p) for i in range(1, doms)]
    for peer in peers:
        pl.semaphore_signal(barrier, inc=1, device_id=peer, device_id_type=MESH)

    first_col = pl.multiple_of(p * (r * LANES), LANES)
    loads = [
        pltpu.make_async_copy(core_hbm.at[:, pl.ds(first_col, r * LANES)], core_v, load_sem.at[0]),
        pltpu.make_async_copy(ion_hbm.at[:, pl.ds(first_col, r * LANES)], ion_v, load_sem.at[1]),
    ]
    for load in loads:
        load.start()

    weight = occ_ref[0, 0]
    lane = lax.broadcasted_iota(jnp.int32, (8, LANES), 1)
    low = lane < GRID
    sign = jnp.where(low, 1.0, -1.0)
    z_first = jnp.bitwise_and(lane, GRID - 1) == 0
    z_last = jnp.bitwise_and(lane, GRID - 1) == GRID - 1
    sub = lax.broadcasted_iota(jnp.int32, (8, LANES), 0)

    def rows_at(k, core, mm):
        return pl.multiple_of(((k * 2 + core) * half + mm) * rows, 8)

    def column_start(x, jj):
        k = x // planes
        xr = x - k * planes
        core = (jj // r) % 2
        extra = jj // (2 * r)
        return ((k * 2 + core) * half + extra) * rows + xr * r + jj % r

    stride = (4 // (2 * r)) * rows

    def put_density(x, plane):
        total = []
        for j in range(8):
            sq = plane[j] * plane[j]
            total.append(weight * (sq + pltpu.roll(sq, GRID, 1)))
        for jj in range(4):
            packed = jnp.where(low, total[2 * jj], total[2 * jj + 1])
            dens[pl.ds(column_start(x, jj), 8, stride=stride), :] = packed

    def stencil(src, x):
        mid = [src[x + 1, j] for j in range(8)]
        before_edge = jnp.where(sub == 0, 0.0, pltpu.roll(mid[7], 1, 0))
        after_edge = jnp.where(sub == 7, 0.0, pltpu.roll(mid[0], 7, 0))
        res = []
        for j in range(8):
            total = src[x, j] + src[x + 2, j]
            total += (mid[j - 1] if j else before_edge) + (mid[j + 1] if j < 7 else after_edge)
            total += jnp.where(z_first, 0.0, pltpu.roll(mid[j], 1, 1))
            total += jnp.where(z_last, 0.0, pltpu.roll(mid[j], LANES - 1, 1))
            res.append(6.0 * mid[j] - total)
        return res, mid

    def loop(start, stop, body, unroll=2):
        def step(i, carry):
            for o in range(unroll):
                body(start + i * unroll + o)
            return carry
        lax.fori_loop(0, (stop - start) // unroll, step, 0)

    def sweep(src, dst):
        def body(x):
            res, _ = stencil(src, x)
            for j in range(8):
                dst[x + 1, j] = res[j]
        loop(0, GRID, body)

    def last_sweep(emit):
        def body(x):
            res, mid = stencil(u3, x)
            plane = []
            for j in range(8):
                odd = H * u1[x + 1, j] - (H**3 / 6) * mid[j]
                even = psi[x + 1, j] - (H**2 / 2) * u2[x + 1, j] + (H**4 / 24) * res[j]
                plane.append(even + sign * pltpu.roll(odd, GRID, 1))
            emit(x, plane)
        return body

    def keep(x, plane):
        for j in range(8):
            psi[x + 1, j] = plane[j]

    def finish(x, plane):
        for j in range(8):
            out_ref[x, pl.ds(j, 8, stride=8), :] = plane[j]

    def phase(t):
        def body(x):
            for jj in range(4):
                v = vbuf[t, pl.ds(column_start(x, jj), 8, stride=stride), :]
                turns = jnp.floor(v * (0.25 / math.pi) + 0.5)
                ang = (v * 0.25 - turns * 3.140625) - turns * (math.pi - 3.140625)
                q = ang * ang
                s = ang * (1.0 + q * (-1 / 6 + q * (1 / 120 + q * (-1 / 5040 + q * (1 / 362880 - q / 39916800)))))
                co = 1.0 + q * (-0.5 + q * (1 / 24 + q * (-1 / 720 + q * (1 / 40320 + q * (-1 / 3628800 + q / 479001600)))))
                sin = 2.0 * s * co
                cos = 1.0 - 2.0 * s * s
                sin_r = pltpu.roll(sin, GRID, 1)
                cos_r = pltpu.roll(cos, GRID, 1)
                for o in range(2):
                    cc = jnp.where(low, cos_r, cos) if o else jnp.where(low, cos, cos_r)
                    ss = jnp.where(low, sin_r, -sin) if o else jnp.where(low, sin, -sin_r)
                    f = psi[x + 1, 2 * jj + o]
                    psi[x + 1, 2 * jj + o] = cc * f + ss * pltpu.roll(f, GRID, 1)
        return body

    zero = jnp.zeros((8, 8, LANES), jnp.float32)
    for ref in (psi, u1, u2, u3):
        ref[0] = zero
        ref[GRID + 1] = zero

    def remote(src, dst, send, recv, peer):
        return pltpu.make_async_remote_copy(
            src_ref=src, dst_ref=dst, send_sem=send, recv_sem=recv,
            device_id=peer, device_id_type=MESH,
        )

    def load_in(x):
        plane = [orb_ref[x, pl.ds(j, 8, stride=8), :] for j in range(8)]
        keep(x, plane)
        put_density(x, plane)

    def density_again(x):
        put_density(x, [psi[x + 1, j] for j in range(8)])

    order = [1, 2, 0, 3] if CHUNKS == 4 else list(range(CHUNKS))
    order = [k for k in (0, CHUNKS - 1)] + [k for k in range(1, CHUNKS - 1)]
    for t in range(STEPS):
        edges = (edges_0, edges_1)[t]
        sends = []

        def go(copy):
            copy.start()
            sends.append(copy)
            return copy

        a_copies = {}
        for k in order:
            loop(k * planes, (k + 1) * planes, density_again if t else load_in)
            if t == 0 and k == order[0]:
                pl.semaphore_wait(barrier, len(peers))
            a_copies[k] = go(remote(
                dens.at[pl.ds(rows_at(k, 1 - c, 0), half * rows)],
                recv_a.at[t, k], a_send.at[t, k], a_recv.at[t, k], (dom, core_peer)))
        sweep(psi, u1)
        b_copies = {}
        for k in order:
            a_copies[k].wait_recv()
            for mm in range(half):
                at = pl.ds(rows_at(k, c, mm), rows)
                dens[at, :] = dens[at, :] + recv_a[t, k, pl.ds(mm * rows, rows), :]
            b_copies[k] = []
            for i in range(far):
                b_copies[k].append(go(remote(
                    dens.at[pl.ds(rows_at(k, c, 2 * i + 1 - b), rows)],
                    recv_b.at[t, k, i], b_send.at[t, k, i], b_recv.at[t, k, i], (dom, x_peer))))
        sweep(u1, u2)
        c_copies = {}
        for k in order:
            for i in range(far):
                b_copies[k][i].wait_recv()
                at = pl.ds(rows_at(k, c, 2 * i + b), rows)
                dens[at, :] = dens[at, :] + recv_b[t, k, i]
            c_copies[k] = []
            for i in range(1, far):
                other, peer = z_peer(i)
                c_copies[k].append(go(remote(
                    dens.at[pl.ds(rows_at(k, c, 2 * other + b), rows)],
                    recv_c.at[t, k, i - 1], c_send.at[t, k, i - 1], c_recv.at[t, k, i - 1], (dom, peer))))
        sweep(u2, u3)
        if t == 0:
            for load in loads:
                load.wait()

        def total_density(k):
            for copy in c_copies[k]:
                copy.wait_recv()
            base = rows_at(k, c, m)
            at = pl.ds(base, rows)
            total = dens[at, :]
            for i in range(far - 1):
                total = total + recv_c[t, k, i]
            dens[at, :] = total
            parts = []
            for rr in range(r):
                parts.append(
                    dens[pl.ds(base + rr, planes, stride=r), :]
                    + core_v[k * planes:(k + 1) * planes, rr * LANES:(rr + 1) * LANES])
            return parts

        z_copies = {}

        def put_potential(k, parts):
            base = rows_at(k, c, m)
            for rr in range(r):
                cols = slice(rr * LANES, (rr + 1) * LANES)
                span = slice(k * planes, (k + 1) * planes)
                root = jnp.exp(jnp.log(parts[rr]) * (1.0 / 3.0))
                root = root - (root - parts[rr] / (root * root)) * (1.0 / 3.0)
                v = ion_v[span, cols] - EXCHANGE_COEF * root
                vbuf[t, pl.ds(base + rr, planes, stride=r), :] = v
                if t == STEPS - 1:
                    pot_ref[span, cols] = v
            z_copies[k] = []
            for i in range(1, far):
                at = pl.ds(base, rows)
                z_copies[k].append(go(remote(
                    vbuf.at[t, at], vbuf.at[t, at],
                    z_send.at[t, k, i - 1], z_recv.at[t, k, i - 1], (dom, z_peer(i)[1]))))

        kept = {}
        for side, k in ((0, 0), (1, CHUNKS - 1)):
            kept[k] = total_density(k)
            span = slice(0, 8) if side == 0 else slice(planes - 8, planes)
            for rr in range(r):
                edges[dom, side, rr] = kept[k][rr][span]
        d_copies = [
            go(remote(edges.at[dom], edges.at[dom],
                      d_send.at[t, i - 1], d_recv.at[t, i - 1], (d_peer(i), p)))
            for i in range(1, doms)
        ]
        for k in range(1, CHUNKS - 1):
            put_potential(k, total_density(k))
        for copy in d_copies:
            copy.wait_recv()
        pos = sub.astype(jnp.float32)
        for side, k in ((0, 0), (1, CHUNKS - 1)):
            width = wid_ref[dom, side].astype(jnp.float32)
            source = nbr_ref[dom, side]
            if side == 0:
                ramp = jnp.maximum(width - pos, 0.0) / (width + 1.0)
            else:
                ramp = jnp.maximum(pos - (BUFFER - width) + 1.0, 0.0) / (width + 1.0)
            parts = []
            for rr in range(r):
                rho = kept[k][rr]
                own = rho[:8] if side == 0 else rho[planes - 8:]
                mixed = (1.0 - ramp) * own + ramp * edges[source, 1 - side, rr]
                both = [mixed, rho[8:]] if side == 0 else [rho[:planes - 8], mixed]
                parts.append(jnp.concatenate(both, axis=0))
            put_potential(k, parts)

        loop(0, GRID, last_sweep(keep))
        back = [k for k in range(1, CHUNKS - 1)] + [0, CHUNKS - 1]
        x_copies = {}
        for k in back:
            x_copies[k] = []
            for i in range(far):
                if i:
                    z_copies[k][i - 1].wait_recv()
                owner = lax.rem(a + far - i, far)
                at = pl.ds(rows_at(k, c, 2 * owner + b), rows)
                x_copies[k].append(go(remote(
                    vbuf.at[t, at], vbuf.at[t, at],
                    x_send.at[t, k, i], x_recv.at[t, k, i], (dom, x_peer))))
        k_copies = {}
        for k in back:
            for copy in x_copies[k]:
                copy.wait_recv()
            at = pl.ds(rows_at(k, c, 0), half * rows)
            k_copies[k] = go(remote(
                vbuf.at[t, at], vbuf.at[t, at],
                k_send.at[t, k], k_recv.at[t, k], (dom, core_peer)))
        for k in back:
            k_copies[k].wait_recv()
            loop(k * planes, (k + 1) * planes, phase(t), 1)
        for copy in sends:
            copy.wait_send()
        sweep(psi, u1)
        sweep(u1, u2)
        sweep(u2, u3)
        loop(0, GRID, last_sweep(keep if t < STEPS - 1 else finish))


def on_device(orbitals, occupations, core_density, ion_potential, neighbors, margin_widths):
    n = lax.axis_size("orb")
    doms = lax.axis_size("dom")
    r = GRID * GRID // (LANES * n)
    planes = GRID // CHUNKS
    rows = planes * r
    half, far = n // 2, n // 4
    total = GRID * GRID * GRID // LANES
    f32 = jnp.float32
    vmem, dma = pltpu.VMEM, pltpu.SemaphoreType.DMA
    state = vmem((GRID + 2, 8, 8, LANES), f32)
    T, K = STEPS, CHUNKS
    out, pot = pl.pallas_call(
        functools.partial(kernel, n, doms),
        out_shape=(
            jax.ShapeDtypeStruct((GRID, GRID, LANES), f32),
            jax.ShapeDtypeStruct((GRID, r * LANES), f32),
        ),
        in_specs=[
            pl.BlockSpec(memory_space=pltpu.VMEM),
            pl.BlockSpec(memory_space=pltpu.SMEM),
            pl.BlockSpec(memory_space=pltpu.SMEM),
            pl.BlockSpec(memory_space=pltpu.SMEM),
            pl.BlockSpec(memory_space=pl.ANY),
            pl.BlockSpec(memory_space=pl.ANY),
        ],
        out_specs=(pl.BlockSpec(memory_space=pltpu.VMEM), pl.BlockSpec(memory_space=pltpu.VMEM)),
        scratch_shapes=[
            state, state, state, state,
            vmem((GRID, r * LANES), f32), vmem((GRID, r * LANES), f32),
            vmem((total, LANES), f32),
            vmem((T, total, LANES), f32),
            vmem((T, K, half * rows, LANES), f32),
            vmem((T, K, far, rows, LANES), f32),
            vmem((T, K, far - 1, rows, LANES), f32),
            vmem((doms, 2, r, BUFFER, LANES), f32),
            vmem((doms, 2, r, BUFFER, LANES), f32),
            dma((2,)),
            dma((T, K)), dma((T, K)),
            dma((T, K, far)), dma((T, K, far)),
            dma((T, K, far - 1)), dma((T, K, far - 1)),
            dma((T, doms - 1)), dma((T, doms - 1)),
            dma((T, K, far - 1)), dma((T, K, far - 1)),
            dma((T, K, far)), dma((T, K, far)),
            dma((T, K)), dma((T, K)),
        ],
        compiler_params=pltpu.CompilerParams(
            collective_id=0, has_side_effects=True, vmem_limit_bytes=40 * 2**20
        ),
    )(orbitals[0, 0], occupations, neighbors, margin_widths, core_density[0], ion_potential[0])
    return out[None, None], pot[None]


def solution(mesh):
    return jax.shard_map(
        on_device,
        mesh=mesh,
        in_specs=(
            P("dom", "orb", None, None, None),
            P("dom", "orb"),
            P("dom", None, None),
            P("dom", None, None),
            P(),
            P(),
        ),
        out_specs=(P("dom", "orb", None, None, None), P("dom", None, "orb")),
        check_vma=False,
    )
```

```python
import functools
import math

import jax
import jax.numpy as jnp
from jax import lax
from jax.experimental import pallas as pl
from jax.experimental.pallas import tpu as pltpu
from jax.sharding import PartitionSpec as P

BUFFER = 8
STEPS = 2
CHUNKS = 4
GRID = 64
LANES = 128
EXCHANGE_COEF = (3.0 / math.pi) ** (1.0 / 3.0)
H = 0.125
MESH = pl.DeviceIdType.MESH


def kernel(
    n, doms,
    orb_ref, occ_ref, nbr_ref, wid_ref, core_hbm, ion_hbm,
    out_ref, pot_ref,
    psi, u1, u2, u3, core_v, ion_v,
    dens, vbuf, recv_a, recv_b, recv_c, edges_0, edges_1,
    load_sem,
    a_send, a_recv, b_send, b_recv, c_send, c_recv,
    d_send, d_recv, z_send, z_recv, x_send, x_recv, k_send, k_recv,
):
    half = n // 2
    far = n // 4
    r = GRID * GRID // (LANES * n)
    planes = GRID // CHUNKS
    rows = planes * r
    dom = lax.axis_index("dom")
    p = lax.axis_index("orb")
    c = lax.rem(p, 2)
    b = lax.rem(p // 2, 2)
    a = p // 4
    m = p // 2
    core_peer = p + 1 - 2 * c
    x_peer = p + 2 - 4 * b

    def z_peer(i):
        other = lax.rem(a + i, far)
        return other, other * 4 + b * 2 + c

    def d_peer(i):
        return lax.rem(dom + i, doms)

    barrier = pltpu.get_barrier_semaphore()
    peers = [(dom, core_peer), (dom, x_peer)]
    peers += [(dom, z_peer(i)[1]) for i in range(1, far)]
    peers += [(d_peer(i), p) for i in range(1, doms)]
    for peer in peers:
        pl.semaphore_signal(barrier, inc=1, device_id=peer, device_id_type=MESH)

    first_col = pl.multiple_of(p * (r * LANES), LANES)
    loads = [
        pltpu.make_async_copy(core_hbm.at[:, pl.ds(first_col, r * LANES)], core_v, load_sem.at[0]),
        pltpu.make_async_copy(ion_hbm.at[:, pl.ds(first_col, r * LANES)], ion_v, load_sem.at[1]),
    ]
    for load in loads:
        load.start()

    weight = occ_ref[0, 0]
    lane = lax.broadcasted_iota(jnp.int32, (8, LANES), 1)
    low = lane < GRID
    sign = jnp.where(low, 1.0, -1.0)
    z_first = jnp.bitwise_and(lane, GRID - 1) == 0
    z_last = jnp.bitwise_and(lane, GRID - 1) == GRID - 1
    sub = lax.broadcasted_iota(jnp.int32, (8, LANES), 0)

    def rows_at(k, core, mm):
        return pl.multiple_of(((k * 2 + core) * half + mm) * rows, 8)

    def column_start(x, jj):
        k = x // planes
        xr = x - k * planes
        core = (jj // r) % 2
        extra = jj // (2 * r)
        return ((k * 2 + core) * half + extra) * rows + xr * r + jj % r

    stride = (4 // (2 * r)) * rows

    def put_density(x, plane):
        total = []
        for j in range(8):
            sq = plane[j] * plane[j]
            total.append(weight * (sq + pltpu.roll(sq, GRID, 1)))
        for jj in range(4):
            packed = jnp.where(low, total[2 * jj], total[2 * jj + 1])
            dens[pl.ds(column_start(x, jj), 8, stride=stride), :] = packed

    def stencil(src, x):
        mid = [src[x + 1, j] for j in range(8)]
        before_edge = jnp.where(sub == 0, 0.0, pltpu.roll(mid[7], 1, 0))
        after_edge = jnp.where(sub == 7, 0.0, pltpu.roll(mid[0], 7, 0))
        res = []
        for j in range(8):
            total = src[x, j] + src[x + 2, j]
            total += (mid[j - 1] if j else before_edge) + (mid[j + 1] if j < 7 else after_edge)
            total += jnp.where(z_first, 0.0, pltpu.roll(mid[j], 1, 1))
            total += jnp.where(z_last, 0.0, pltpu.roll(mid[j], LANES - 1, 1))
            res.append(6.0 * mid[j] - total)
        return res, mid

    def loop(start, stop, body, unroll=2):
        def step(i, carry):
            for o in range(unroll):
                body(start + i * unroll + o)
            return carry
        lax.fori_loop(0, (stop - start) // unroll, step, 0)

    def sweep(src, dst):
        def body(x):
            res, _ = stencil(src, x)
            for j in range(8):
                dst[x + 1, j] = res[j]
        loop(0, GRID, body)

    def last_sweep(emit):
        def body(x):
            res, mid = stencil(u3, x)
            plane = []
            for j in range(8):
                odd = H * u1[x + 1, j] - (H**3 / 6) * mid[j]
                even = psi[x + 1, j] - (H**2 / 2) * u2[x + 1, j] + (H**4 / 24) * res[j]
                plane.append(even + sign * pltpu.roll(odd, GRID, 1))
            emit(x, plane)
        return body

    def keep(x, plane):
        for j in range(8):
            psi[x + 1, j] = plane[j]

    def finish(x, plane):
        for j in range(8):
            out_ref[x, pl.ds(j, 8, stride=8), :] = plane[j]

    def phase(t):
        def body(x):
            for jj in range(4):
                v = vbuf[t, pl.ds(column_start(x, jj), 8, stride=stride), :]
                turns = jnp.floor(v * (0.25 / math.pi) + 0.5)
                ang = (v * 0.25 - turns * 3.140625) - turns * (math.pi - 3.140625)
                q = ang * ang
                s = ang * (1.0 + q * (-1 / 6 + q * (1 / 120 + q * (-1 / 5040 + q * (1 / 362880 - q / 39916800)))))
                co = 1.0 + q * (-0.5 + q * (1 / 24 + q * (-1 / 720 + q * (1 / 40320 + q * (-1 / 3628800 + q / 479001600)))))
                sin = 2.0 * s * co
                cos = 1.0 - 2.0 * s * s
                sin_r = pltpu.roll(sin, GRID, 1)
                cos_r = pltpu.roll(cos, GRID, 1)
                for o in range(2):
                    cc = jnp.where(low, cos_r, cos) if o else jnp.where(low, cos, cos_r)
                    ss = jnp.where(low, sin_r, -sin) if o else jnp.where(low, sin, -sin_r)
                    f = psi[x + 1, 2 * jj + o]
                    psi[x + 1, 2 * jj + o] = cc * f + ss * pltpu.roll(f, GRID, 1)
        return body

    zero = jnp.zeros((8, 8, LANES), jnp.float32)
    for ref in (psi, u1, u2, u3):
        ref[0] = zero
        ref[GRID + 1] = zero

    def remote(src, dst, send, recv, peer):
        return pltpu.make_async_remote_copy(
            src_ref=src, dst_ref=dst, send_sem=send, recv_sem=recv,
            device_id=peer, device_id_type=MESH,
        )

    def load_in(x):
        plane = [orb_ref[x, pl.ds(j, 8, stride=8), :] for j in range(8)]
        keep(x, plane)
        put_density(x, plane)

    def density_again(x):
        put_density(x, [psi[x + 1, j] for j in range(8)])

    order = [1, 2, 0, 3] if CHUNKS == 4 else list(range(CHUNKS))
    order = [k for k in (0, CHUNKS - 1)] + [k for k in range(1, CHUNKS - 1)]
    for t in range(STEPS):
        edges = (edges_0, edges_1)[t]
        sends = []

        def go(copy):
            copy.start()
            sends.append(copy)
            return copy

        a_copies = {}
        b_copies = {}

        def start_x(k):
            a_copies[k].wait_recv()
            for mm in range(half):
                at = pl.ds(rows_at(k, c, mm), rows)
                dens[at, :] = dens[at, :] + recv_a[t, k, pl.ds(mm * rows, rows), :]
            b_copies[k] = []
            for i in range(far):
                b_copies[k].append(go(remote(
                    dens.at[pl.ds(rows_at(k, c, 2 * i + 1 - b), rows)],
                    recv_b.at[t, k, i], b_send.at[t, k, i], b_recv.at[t, k, i], (dom, x_peer))))

        for place, k in enumerate(order):
            loop(k * planes, (k + 1) * planes, density_again if t else load_in)
            if t == 0 and k == order[0]:
                pl.semaphore_wait(barrier, len(peers))
            a_copies[k] = go(remote(
                dens.at[pl.ds(rows_at(k, 1 - c, 0), half * rows)],
                recv_a.at[t, k], a_send.at[t, k], a_recv.at[t, k], (dom, core_peer)))
            if place:
                start_x(order[place - 1])
        start_x(order[-1])
        sweep(psi, u1)
        c_copies = {}
        for k in order:
            for i in range(far):
                b_copies[k][i].wait_recv()
                at = pl.ds(rows_at(k, c, 2 * i + b), rows)
                dens[at, :] = dens[at, :] + recv_b[t, k, i]
            c_copies[k] = []
            for i in range(1, far):
                other, peer = z_peer(i)
                c_copies[k].append(go(remote(
                    dens.at[pl.ds(rows_at(k, c, 2 * other + b), rows)],
                    recv_c.at[t, k, i - 1], c_send.at[t, k, i - 1], c_recv.at[t, k, i - 1], (dom, peer))))
        sweep(u1, u2)
        sweep(u2, u3)
        if t == 0:
            for load in loads:
                load.wait()

        def total_density(k):
            for copy in c_copies[k]:
                copy.wait_recv()
            base = rows_at(k, c, m)
            at = pl.ds(base, rows)
            total = dens[at, :]
            for i in range(far - 1):
                total = total + recv_c[t, k, i]
            dens[at, :] = total
            parts = []
            for rr in range(r):
                parts.append(
                    dens[pl.ds(base + rr, planes, stride=r), :]
                    + core_v[k * planes:(k + 1) * planes, rr * LANES:(rr + 1) * LANES])
            return parts

        z_copies = {}

        def put_potential(k, parts):
            base = rows_at(k, c, m)
            for rr in range(r):
                cols = slice(rr * LANES, (rr + 1) * LANES)
                span = slice(k * planes, (k + 1) * planes)
                root = jnp.exp(jnp.log(parts[rr]) * (1.0 / 3.0))
                root = root - (root - parts[rr] / (root * root)) * (1.0 / 3.0)
                v = ion_v[span, cols] - EXCHANGE_COEF * root
                vbuf[t, pl.ds(base + rr, planes, stride=r), :] = v
                if t == STEPS - 1:
                    pot_ref[span, cols] = v
            z_copies[k] = []
            for i in range(1, far):
                at = pl.ds(base, rows)
                z_copies[k].append(go(remote(
                    vbuf.at[t, at], vbuf.at[t, at],
                    z_send.at[t, k, i - 1], z_recv.at[t, k, i - 1], (dom, z_peer(i)[1]))))

        kept = {}
        for side, k in ((0, 0), (1, CHUNKS - 1)):
            kept[k] = total_density(k)
            span = slice(0, 8) if side == 0 else slice(planes - 8, planes)
            for rr in range(r):
                edges[dom, side, rr] = kept[k][rr][span]
        d_copies = [
            go(remote(edges.at[dom], edges.at[dom],
                      d_send.at[t, i - 1], d_recv.at[t, i - 1], (d_peer(i), p)))
            for i in range(1, doms)
        ]
        for k in range(1, CHUNKS - 1):
            put_potential(k, total_density(k))
        for copy in d_copies:
            copy.wait_recv()
        pos = sub.astype(jnp.float32)
        for side, k in ((0, 0), (1, CHUNKS - 1)):
            width = wid_ref[dom, side].astype(jnp.float32)
            source = nbr_ref[dom, side]
            if side == 0:
                ramp = jnp.maximum(width - pos, 0.0) / (width + 1.0)
            else:
                ramp = jnp.maximum(pos - (BUFFER - width) + 1.0, 0.0) / (width + 1.0)
            parts = []
            for rr in range(r):
                rho = kept[k][rr]
                own = rho[:8] if side == 0 else rho[planes - 8:]
                mixed = (1.0 - ramp) * own + ramp * edges[source, 1 - side, rr]
                both = [mixed, rho[8:]] if side == 0 else [rho[:planes - 8], mixed]
                parts.append(jnp.concatenate(both, axis=0))
            put_potential(k, parts)

        loop(0, GRID, last_sweep(keep))
        back = [k for k in range(1, CHUNKS - 1)] + [0, CHUNKS - 1]
        x_copies = {}
        for k in back:
            x_copies[k] = []
            for i in range(far):
                if i:
                    z_copies[k][i - 1].wait_recv()
                owner = lax.rem(a + far - i, far)
                at = pl.ds(rows_at(k, c, 2 * owner + b), rows)
                x_copies[k].append(go(remote(
                    vbuf.at[t, at], vbuf.at[t, at],
                    x_send.at[t, k, i], x_recv.at[t, k, i], (dom, x_peer))))
        k_copies = {}
        for k in back:
            for copy in x_copies[k]:
                copy.wait_recv()
            at = pl.ds(rows_at(k, c, 0), half * rows)
            k_copies[k] = go(remote(
                vbuf.at[t, at], vbuf.at[t, at],
                k_send.at[t, k], k_recv.at[t, k], (dom, core_peer)))
        for k in back:
            k_copies[k].wait_recv()
            loop(k * planes, (k + 1) * planes, phase(t), 2)
        for copy in sends:
            copy.wait_send()
        sweep(psi, u1)
        sweep(u1, u2)
        sweep(u2, u3)
        loop(0, GRID, last_sweep(keep if t < STEPS - 1 else finish))


def on_device(orbitals, occupations, core_density, ion_potential, neighbors, margin_widths):
    n = lax.axis_size("orb")
    doms = lax.axis_size("dom")
    r = GRID * GRID // (LANES * n)
    planes = GRID // CHUNKS
    rows = planes * r
    half, far = n // 2, n // 4
    total = GRID * GRID * GRID // LANES
    f32 = jnp.float32
    vmem, dma = pltpu.VMEM, pltpu.SemaphoreType.DMA
    state = vmem((GRID + 2, 8, 8, LANES), f32)
    T, K = STEPS, CHUNKS
    out, pot = pl.pallas_call(
        functools.partial(kernel, n, doms),
        out_shape=(
            jax.ShapeDtypeStruct((GRID, GRID, LANES), f32),
            jax.ShapeDtypeStruct((GRID, r * LANES), f32),
        ),
        in_specs=[
            pl.BlockSpec(memory_space=pltpu.VMEM),
            pl.BlockSpec(memory_space=pltpu.SMEM),
            pl.BlockSpec(memory_space=pltpu.SMEM),
            pl.BlockSpec(memory_space=pltpu.SMEM),
            pl.BlockSpec(memory_space=pl.ANY),
            pl.BlockSpec(memory_space=pl.ANY),
        ],
        out_specs=(pl.BlockSpec(memory_space=pltpu.VMEM), pl.BlockSpec(memory_space=pltpu.VMEM)),
        scratch_shapes=[
            state, state, state, state,
            vmem((GRID, r * LANES), f32), vmem((GRID, r * LANES), f32),
            vmem((total, LANES), f32),
            vmem((T, total, LANES), f32),
            vmem((T, K, half * rows, LANES), f32),
            vmem((T, K, far, rows, LANES), f32),
            vmem((T, K, far - 1, rows, LANES), f32),
            vmem((doms, 2, r, BUFFER, LANES), f32),
            vmem((doms, 2, r, BUFFER, LANES), f32),
            dma((2,)),
            dma((T, K)), dma((T, K)),
            dma((T, K, far)), dma((T, K, far)),
            dma((T, K, far - 1)), dma((T, K, far - 1)),
            dma((T, doms - 1)), dma((T, doms - 1)),
            dma((T, K, far - 1)), dma((T, K, far - 1)),
            dma((T, K, far)), dma((T, K, far)),
            dma((T, K)), dma((T, K)),
        ],
        compiler_params=pltpu.CompilerParams(
            collective_id=0, has_side_effects=True, vmem_limit_bytes=40 * 2**20
        ),
    )(orbitals[0, 0], occupations, neighbors, margin_widths, core_density[0], ion_potential[0])
    return out[None, None], pot[None]


def solution(mesh):
    return jax.shard_map(
        on_device,
        mesh=mesh,
        in_specs=(
            P("dom", "orb", None, None, None),
            P("dom", "orb"),
            P("dom", None, None),
            P("dom", None, None),
            P(),
            P(),
        ),
        out_specs=(P("dom", "orb", None, None, None), P("dom", None, "orb")),
        check_vma=False,
    )
```
